256 devices in a mesh: dp: 8 (over z_hi, core), tensor: 32 (over x, z_lo, y).
Axes of the slice: x: 4, y: 4, z: 8 (z_hi: 4, z_lo: 2; z = z_hi * 2 + z_lo), core: 2. Of those that a mesh axis runs over, the one named last changes fastest.
Arguments:
- d_out: bfloat16 [1024, 8192], P('dp', 'tensor'), may hold values from -6 to 6
- gate_act: bfloat16 [1024, 14336], P('dp', 'tensor'), may hold values from -6 to 6
- up_act: bfloat16 [1024, 14336], P('dp', 'tensor'), may hold values from -6 to 6
- gate_weight: bfloat16 [8192, 14336], P('dp', 'tensor'), may hold values from -0.0625 to 0.0625
- up_weight: bfloat16 [8192, 14336], P('dp', 'tensor'), may hold values from -0.0625 to 0.0625
- down_weight: bfloat16 [8192, 14336], P('dp', 'tensor'), may hold values from -0.046875 to 0.046875
- momentum: float32 [8192, 14336], P('dp', 'tensor'), may hold values from -12 to 12
Outputs:
- d_in: bfloat16 [1024, 8192], P('tensor', 'dp')
- direction: bfloat16 [8192, 14336], P('dp', 'tensor')
- new_momentum: float32 [8192, 14336], P('dp', 'tensor')
The draws below stay inside these ranges and needn't reach their ends.
All inputs are finite; a program needn't handle non-finite values.
Results may differ from the reference program's by a relative error of at most 0.0049.
Values may be sent and summed in bfloat16 or wider, within the bound.
No kernel may reach another device: no remote copies, remote signals or barrier semaphores. Data moves between devices by JAX's collectives and lax.ppermute only.
A program may use at most 128 MiB of HBM per device.

```python
import jax
import jax.numpy as jnp
from jax import lax

D = 8192
TOK_DEV = 128
HID = 14336
TOKENS = 1024
N_DP = 8


def with_spikes(entries, stream_key, source, target, shards_of, factor):
    owner, partner = [(jnp.arange(entries.shape[dim]) // (entries.shape[dim] // shards_of)).reshape([-1 if axis == dim else 1 for axis in range(entries.ndim)]) for dim in (source, target)]
    chosen = jax.random.permutation(stream_key, shards_of)[partner]
    strong = (owner == chosen) | (owner == (partner + shards_of // 2) % shards_of)
    return jnp.where(strong, factor * entries, entries)


def steps_of(rng, shape, pieces, smallest, largest):
    def one(position, shards_of):
        steps = jax.random.uniform(jax.random.fold_in(jax.random.fold_in(rng, 6), position), (shards_of,), jnp.float32, smallest / len(pieces), largest / len(pieces))
        return jnp.repeat(jnp.exp(steps), shape[position] // shards_of).reshape((-1,) + (1,) * (len(shape) - position - 1))

    gain = one(*pieces[0])
    for cut in pieces[1:]:
        gain = gain * one(*cut)
    return gain


def bell_draw(rng, extent, width, bound, shards=(), kind=jnp.bfloat16):
    array = width * jax.random.normal(rng, extent, jnp.float32)
    if shards:
        array = array * steps_of(rng, extent, shards, -0.22, 0.18)
    return jnp.clip(array, -bound, bound).astype(kind)


def noise_with(own_key, shape, scale, bound, pieces, heavy, held_as=jnp.bfloat16):
    entries = scale * jax.random.normal(own_key, shape, jnp.float32)
    if pieces:
        entries = entries * steps_of(own_key, shape, pieces, -0.22, 0.18)
    return jnp.clip(with_spikes(entries, jax.random.fold_in(own_key, 3), *heavy), -bound, bound).astype(held_as)


def setup_inputs(seed: int = 0) -> dict:
    key_list = jax.random.split(jax.random.key(seed), 8)
    return {
        "d_out": noise_with(key_list[0], (TOKENS, D), 1.0, 6.0, ((0, 8), (1, 32)), (0, 1, 32, 2.75)),
        "gate_act": bell_draw(key_list[1], (TOKENS, HID), 1.0, 6.0, ((0, 8), (1, 32))),
        "up_act": noise_with(key_list[2], (TOKENS, HID), 1.0, 6.0, ((0, 8), (1, 32)), (1, 0, 32, 2.75)),
        "gate_weight": bell_draw(key_list[3], (D, HID), D ** -0.5, 0.0625, ((0, 8), (1, 32))),
        "up_weight": bell_draw(key_list[4], (D, HID), D ** -0.5, 0.0625, ((0, 8), (1, 32))),
        "down_weight": bell_draw(key_list[5], (D, HID), HID ** -0.5, 0.046875, ((0, 8), (1, 32))),
        "momentum": bell_draw(key_list[6], (D, HID), 2.0, 12.0, ((0, 8), (1, 32)), jnp.float32),
    }


def reference(d_out, gate_act, up_act, gate_weight, up_weight, down_weight, momentum):
    gate_full = gate_act.astype(jnp.float32)
    up_full = up_act.astype(jnp.float32)
    sigma = jax.nn.sigmoid(gate_full)
    swish = gate_full * sigma
    hidden = (swish * up_full).astype(jnp.bfloat16)
    d_hidden = jnp.dot(d_out, down_weight, preferred_element_type=jnp.float32)
    d_up = (d_hidden * swish).astype(jnp.bfloat16)
    d_gate = (d_hidden * up_full * sigma * (1.0 + gate_full * (1.0 - sigma))).astype(jnp.bfloat16)
    d_in = (jnp.dot(d_gate, gate_weight.T, preferred_element_type=jnp.float32)
            + jnp.dot(d_up, up_weight.T, preferred_element_type=jnp.float32)).astype(jnp.bfloat16)

    def add_group(total, index):
        start = (index * TOK_DEV).astype(jnp.int32)
        columns = lax.dynamic_slice_in_dim(d_out, start, TOK_DEV, 0)
        acts = lax.dynamic_slice_in_dim(hidden, start, TOK_DEV, 0)
        term = lax.dot_general(columns, acts, (((0,), (0,)), ((), ())), preferred_element_type=jnp.float32)
        return total + term, None

    grad_sum, _ = lax.scan(add_group, jnp.zeros((D, HID), jnp.float32), jnp.arange(N_DP, dtype=jnp.int32))
    grad_mean = grad_sum / N_DP
    direction = (0.9 * momentum + 0.1 * grad_mean).astype(jnp.bfloat16)
    new_momentum = 0.99 * momentum + 0.01 * grad_mean
    return d_in, direction, new_momentum
```

```python
import jax
import jax.numpy as jnp
import numpy as np
from jax import lax
from jax.sharding import Mesh, PartitionSpec as P

AXES = ("zh", "co", "x", "zl", "y")
SIZES = (4, 2, 4, 2, 4)
DP = ("zh", "co")
TENSOR = ("x", "zl", "y")


def pairs(move):
    found = []
    for source in range(256):
        place = [int(v) for v in np.unravel_index(source, SIZES)]
        found.append((source, int(np.ravel_multi_index(move(*place), SIZES))))
    return found


TRANSPOSE = pairs(lambda zh, co, x, zl, y: (x, zl, zh, co, y))


def body(d_out, gate_act, up_act, gate_weight, up_weight, down_weight, momentum):
    turned = lax.ppermute(d_out, AXES, TRANSPOSE)
    spread = jnp.broadcast_to(turned[None], (32, 128, 256))
    slots = lax.all_to_all(spread, TENSOR, split_axis=0, concat_axis=0, tiled=True)
    exchanged = slots.reshape(8, 4, 128, 256).transpose(0, 2, 1, 3).reshape(1024, 1024)
    all_gate = lax.all_gather(gate_act, DP, axis=0, tiled=True).astype(jnp.float32)
    all_up = lax.all_gather(up_act, DP, axis=0, tiled=True).astype(jnp.float32)
    sigma = jax.nn.sigmoid(all_gate)
    swish = all_gate * sigma
    hidden = (swish * all_up).astype(jnp.bfloat16)

    partial = jnp.dot(exchanged, down_weight, preferred_element_type=jnp.float32)
    parts = lax.all_to_all(
        partial.astype(jnp.bfloat16).reshape(8, 128, 448), DP, split_axis=0, concat_axis=0, tiled=True
    )
    mine = jnp.sum(parts.astype(jnp.float32), axis=0).astype(jnp.bfloat16)
    d_hidden = lax.all_gather(mine, DP, axis=0, tiled=True).astype(jnp.float32)
    d_up = (d_hidden * swish).astype(jnp.bfloat16)
    d_gate = (d_hidden * all_up * sigma * (1.0 + all_gate * (1.0 - sigma))).astype(jnp.bfloat16)
    first = lax.dot_general(
        d_gate, gate_weight, (((1,), (1,)), ((), ())), preferred_element_type=jnp.float32
    )
    second = lax.dot_general(
        d_up, up_weight, (((1,), (1,)), ((), ())), preferred_element_type=jnp.float32
    )
    slices = lax.all_to_all(
        (first + second).astype(jnp.bfloat16).reshape(32, 32, 1024),
        TENSOR,
        split_axis=0,
        concat_axis=0,
        tiled=True,
    )
    d_in = jnp.sum(slices.astype(jnp.float32), axis=0).astype(jnp.bfloat16)

    grad_sum = lax.dot_general(
        exchanged, hidden, (((0,), (0,)), ((), ())), preferred_element_type=jnp.float32
    )
    grad_mean = grad_sum / 8
    direction = (0.9 * momentum + 0.1 * grad_mean).astype(jnp.bfloat16)
    new_momentum = 0.99 * momentum + 0.01 * grad_mean
    return d_in, direction, new_momentum


def solution(mesh):
    fine = Mesh(mesh.devices.reshape(SIZES), AXES)
    both = P(DP, TENSOR)
    return jax.shard_map(
        body,
        mesh=fine,
        in_specs=(both,) * 7,
        out_specs=(P(TENSOR, DP), both, both),
        check_vma=False,
    )
```

```python
import jax
import jax.numpy as jnp
import numpy as np
from jax import lax
from jax.experimental import pallas as pl
from jax.experimental.pallas import tpu as pltpu
from jax.sharding import Mesh, PartitionSpec as P

AXES = ("zh", "co", "x", "zl", "y")
SIZES = (4, 2, 4, 2, 4)
DP = ("zh", "co")
TENSOR = ("x", "zl", "y")
CUTS = 1
PART = 128 // CUTS
ROWS = 32 // CUTS
HALF = 224
F32, BF16 = jnp.float32, jnp.bfloat16
PLACE = pl.BlockSpec(memory_space=pltpu.SMEM)
WHOLE = pl.BlockSpec(memory_space=pltpu.VMEM)
LIMIT = 16 * 1024 * 1024


def pairs(move):
    found = []
    for source in range(256):
        place = [int(v) for v in np.unravel_index(source, SIZES)]
        found.append((source, int(np.ravel_multi_index(move(*place), SIZES))))
    return found


TRANSPOSE = pairs(lambda zh, co, x, zl, y: (x, zl, zh, co, y))
OTHER_CORE = pairs(lambda zh, co, x, zl, y: (zh, 1 - co, x, zl, y))
NEXT_CHIP = pairs(lambda zh, co, x, zl, y: (zh, co, x, 1 - zl, y))
ALONG = [None] + [
    pairs(lambda zh, co, x, zl, y, k=k: ((zh + k) % 4, co, x, zl, y)) for k in (1, 2, 3)
]


def shape(*dims, kind=F32):
    return jax.ShapeDtypeStruct(dims, kind)


def call(kernel, out_shape, operands, scratch=(), cost=None):
    return pl.pallas_call(
        kernel,
        out_shape=out_shape,
        in_specs=[PLACE] + [WHOLE] * (len(operands) - 1),
        out_specs=jax.tree.map(lambda _: WHOLE, out_shape),
        scratch_shapes=list(scratch),
        compiler_params=pltpu.CompilerParams(vmem_limit_bytes=LIMIT),
        cost_estimate=cost,
    )(*operands)


def product_kernel(place, slots, weight, keep, give):
    core = place[1]
    right = jnp.concatenate([slots[0, y].reshape(2 * PART, 256) for y in range(4)], axis=1)
    for which, out in ((core, keep), (1 - core, give)):
        left = weight[pl.ds(pl.multiple_of(which * HALF, 32), HALF), :]
        out[0] = lax.dot_general(
            left, right, (((1,), (1,)), ((), ())), preferred_element_type=F32
        )


def first_product(place, slots, weight):
    part = pl.BlockSpec((1, HALF, 2 * PART), lambda zh: (zh, 0, 0))
    return pl.pallas_call(
        product_kernel,
        grid=(4,),
        out_shape=(shape(4, HALF, 2 * PART),) * 2,
        in_specs=[
            PLACE,
            pl.BlockSpec((1, 4, 2, PART, 256), lambda zh: (zh, 0, 0, 0, 0)),
            pl.BlockSpec((448, 1024), lambda zh: (0, 0)),
        ],
        out_specs=[part, part],
        compiler_params=pltpu.CompilerParams(vmem_limit_bytes=LIMIT),
    )(place, slots, weight)


def split_kernel(place, keep, got, own, one, two, three):
    zh = place[0]
    own[...] = keep[zh] + got[zh]
    for k, out in ((1, one), (2, two), (3, three)):
        to = lax.rem(zh + k, 4)
        out[...] = (keep[to] + got[to]).astype(BF16)


def factor_kernel(place, mine, other, hidden, by_gate, by_up):
    zh, core = place[0], place[1]
    for k in range(4):
        group = lax.rem(zh + 4 - k, 4)
        first = jnp.where(core == 0, mine[k], other[k])
        second = jnp.where(core == 0, other[k], mine[k])
        for cut in range(CUTS):
            lanes = slice(cut * PART, (cut + 1) * PART)
            both = jnp.concatenate([first[:, :, lanes], second[:, :, lanes]], axis=2)
            for half in range(2):
                units = slice(half * HALF, (half + 1) * HALF)
                gate, up = both[0, units].astype(F32), both[1, units].astype(F32)
                sigma = jax.nn.sigmoid(gate)
                swish = gate * sigma
                hidden[cut, group, units] = (swish * up).astype(BF16)

                @pl.when(core == half)
                def _():
                    by_up[cut, group] = swish
                    by_gate[cut, group] = up * sigma * (1.0 + gate * (1.0 - sigma))


def back_kernel(place, mine, by_gate, by_up, out):
    zh = place[0]
    for k in range(4):
        group = lax.rem(zh + 4 - k, 4)
        block = mine[k].astype(F32)
        both = jnp.concatenate([block * by_gate[group], block * by_up[group]], axis=0)
        out[group, :, :448] = both.astype(BF16).T


def input_kernel(place, mine, other, gate_weight, up_weight, out):
    core = place[1]
    total = None
    for held, which in ((mine, core), (other, 1 - core)):
        units = pl.ds(pl.multiple_of(which * HALF, 32), HALF)
        right = jnp.concatenate([gate_weight[units], up_weight[units]], axis=0)
        term = jnp.dot(held[:, :, :448].reshape(8 * PART, 448), right, preferred_element_type=F32)
        total = term if total is None else total + term
    out[...] = total.astype(BF16).reshape(4, 2, PART, 256)


def second_product(place, mine, other, gate_weight, up_weight):
    held = pl.BlockSpec((4, 2 * PART, 512), lambda n: (0, 0, 0))
    weight = pl.BlockSpec((448, 256), lambda n: (0, n))
    return pl.pallas_call(
        input_kernel,
        grid=(4,),
        out_shape=shape(4, 2, PART, 1024, kind=BF16),
        in_specs=[PLACE, held, held, weight, weight],
        out_specs=pl.BlockSpec((4, 2, PART, 256), lambda n: (0, 0, 0, n)),
        compiler_params=pltpu.CompilerParams(vmem_limit_bytes=LIMIT),
    )(place, mine, other, gate_weight, up_weight)


def momentum_kernel(*refs):
    slots, (hidden, momentum, direction, new_momentum) = refs[:CUTS], refs[CUTS:]
    total = None
    for cut in range(CUTS):
        left = jnp.concatenate([hidden[cut, zh] for zh in range(4)], axis=1)
        term = jnp.dot(left, slots[cut][:, 0].reshape(8 * PART, 256), preferred_element_type=F32)
        total = term if total is None else total + term
    mean = total * 0.125
    direction[...] = (0.9 * momentum[...] + 0.1 * mean).astype(BF16)
    new_momentum[...] = 0.99 * momentum[...] + 0.01 * mean


def sum_kernel(slices, out):
    total = slices[0].astype(F32)
    for i in range(1, 32):
        total = total + slices[i].astype(F32)
    out[...] = total.astype(BF16)


def exchange(slots, axes):
    return lax.all_to_all(slots, axes, split_axis=0, concat_axis=0, tiled=True)


def around(blocks):
    return [lax.ppermute(block, AXES, ALONG[k + 1]) for k, block in enumerate(blocks)]


def body(d_out, gate_act, up_act, gate_weight, up_weight, down_weight, momentum):
    place = jnp.stack([lax.axis_index("zh"), lax.axis_index("co")]).astype(jnp.int32)
    turned = lax.ppermute(d_out, AXES, TRANSPOSE)
    acts = jnp.stack([gate_act.T, up_act.T])
    if CUTS > 1:
        acts = acts.reshape(2, 448, 4, CUTS, ROWS).swapaxes(2, 3).reshape(2, 448, 128)
    acts, turned = lax.optimization_barrier((acts, turned))
    low = lax.axis_index("zl")
    beside = lax.ppermute(turned, AXES, NEXT_CHIP)
    pair = jnp.stack([jnp.where(low == 0, turned, beside), jnp.where(low == 0, beside, turned)])
    pair = pair.reshape(2, 4, CUTS, ROWS, 256)
    blocks = []
    for cut in range(CUTS):
        spread = jnp.broadcast_to(pair[:, :, cut].reshape(1, 2, PART, 256), (16, 2, PART, 256))
        blocks.append(exchange(spread, ("x", "y")).reshape(4, 4, 2, PART, 256))

    groups = around([acts] * 3)
    blocks[0], *groups = lax.optimization_barrier((blocks[0], *groups))
    mine = jnp.stack([acts] + groups)
    other = lax.ppermute(mine, AXES, OTHER_CORE)
    hidden, by_gate, by_up = call(
        factor_kernel,
        (
            shape(CUTS, 4, 448, 2 * PART, kind=BF16),
            shape(CUTS, 4, HALF, 2 * PART),
            shape(CUTS, 4, HALF, 2 * PART),
        ),
        (place, mine, other),
    )

    results = []
    for cut in range(CUTS):
        keep, give = first_product(place, blocks[cut], down_weight.T)
        got = lax.ppermute(give, AXES, OTHER_CORE)
        own, *away = call(
            split_kernel,
            (shape(HALF, 2 * PART),) + (shape(HALF, 2 * PART, kind=BF16),) * 3,
            (place, keep, got),
        )
        total = own
        for block in around(away):
            total = total + block.astype(F32)
        total = total.astype(BF16)
        mine = jnp.stack([total] + around([total] * 3))
        mine = call(
            back_kernel,
            shape(4, 2 * PART, 512, kind=BF16),
            (place, mine, by_gate[cut], by_up[cut]),
        )
        other = lax.ppermute(mine, AXES, OTHER_CORE)
        partial = second_product(place, mine, other, gate_weight.T, up_weight.T)
        slices = exchange(partial.reshape(32, ROWS, 1024), TENSOR)
        results.append(
            pl.pallas_call(
                sum_kernel,
                out_shape=shape(ROWS, 1024, kind=BF16),
            )(slices)
        )
    d_in = jnp.concatenate(results, axis=0)

    direction, new_momentum = pl.pallas_call(
        momentum_kernel,
        grid=(4,),
        out_shape=(shape(448, 1024, kind=BF16), shape(448, 1024)),
        in_specs=[pl.BlockSpec((4, 1, 2, PART, 256), lambda y: (0, y, 0, 0, 0))] * CUTS
        + [
            pl.BlockSpec((CUTS, 4, 448, 2 * PART), lambda y: (0, 0, 0, 0)),
            pl.BlockSpec((448, 256), lambda y: (0, y)),
        ],
        out_specs=[pl.BlockSpec((448, 256), lambda y: (0, y))] * 2,
        compiler_params=pltpu.CompilerParams(vmem_limit_bytes=LIMIT),
    )(*blocks, hidden, momentum.T)
    return d_in, direction.T, new_momentum.T


def solution(mesh):
    fine = Mesh(mesh.devices.reshape(SIZES), AXES)
    both = P(DP, TENSOR)
    return jax.shard_map(
        body,
        mesh=fine,
        in_specs=(both,) * 7,
        out_specs=(P(TENSOR, DP), both, both),
        check_vma=False,
    )
```

```python
import jax
import jax.numpy as jnp
import numpy as np
from jax import lax
from jax.experimental import pallas as pl
from jax.experimental.pallas import tpu as pltpu
from jax.sharding import Mesh, PartitionSpec as P

AXES = ("zh", "co", "x", "zl", "y")
SIZES = (4, 2, 4, 2, 4)
DP = ("zh", "co")
TENSOR = ("x", "zl", "y")
CUTS = 1
PART = 128 // CUTS
ROWS = 32 // CUTS
HALF = 224
F32, BF16 = jnp.float32, jnp.bfloat16
PLACE = pl.BlockSpec(memory_space=pltpu.SMEM)
WHOLE = pl.BlockSpec(memory_space=pltpu.VMEM)
LIMIT = 16 * 1024 * 1024


def pairs(move):
    found = []
    for source in range(256):
        place = [int(v) for v in np.unravel_index(source, SIZES)]
        found.append((source, int(np.ravel_multi_index(move(*place), SIZES))))
    return found


TRANSPOSE = pairs(lambda zh, co, x, zl, y: (x, zl, (zh + 2) % 4, co, y))
OTHER_CORE = pairs(lambda zh, co, x, zl, y: (zh, 1 - co, x, zl, y))
NEXT_CHIP = pairs(lambda zh, co, x, zl, y: (zh, co, x, 1 - zl, y))
ALONG = [None] + [
    pairs(lambda zh, co, x, zl, y, k=k: ((zh + k) % 4, co, x, zl, y)) for k in (1, 2, 3)
]


def shape(*dims, kind=F32):
    return jax.ShapeDtypeStruct(dims, kind)


def call(kernel, out_shape, operands, scratch=(), cost=None):
    return pl.pallas_call(
        kernel,
        out_shape=out_shape,
        in_specs=[PLACE] + [WHOLE] * (len(operands) - 1),
        out_specs=jax.tree.map(lambda _: WHOLE, out_shape),
        scratch_shapes=list(scratch),
        compiler_params=pltpu.CompilerParams(vmem_limit_bytes=LIMIT),
        cost_estimate=cost,
    )(*operands)


def product_kernel(place, slots, weight, keep, give, held, sems):
    core = place[1]
    copies = [pltpu.make_async_copy(slots.at[zh ^ 2], held.at[zh], sems.at[zh]) for zh in range(4)]
    for copy in copies:
        copy.start()
    for zh, copy in enumerate(copies):
        copy.wait()
        right = jnp.concatenate([held[zh, y].reshape(2 * PART, 256) for y in range(4)], axis=1)
        for which, out in ((core, keep), (1 - core, give)):
            left = weight[pl.ds(pl.multiple_of(which * HALF, 32), HALF), :]
            out[zh] = lax.dot_general(
                left, right, (((1,), (1,)), ((), ())), preferred_element_type=F32
            )


def first_product(place, slots, weight):
    return pl.pallas_call(
        product_kernel,
        out_shape=(shape(4, HALF, 2 * PART),) * 2,
        in_specs=[PLACE, pl.BlockSpec(memory_space=pl.ANY), WHOLE],
        out_specs=[WHOLE] * 2,
        scratch_shapes=[pltpu.VMEM((4, 4, 2, PART, 256), BF16), pltpu.SemaphoreType.DMA((4,))],
        compiler_params=pltpu.CompilerParams(vmem_limit_bytes=LIMIT),
    )(place, slots, weight)


def split_kernel(place, keep, got, own, one, two, three):
    zh = place[0]
    own[...] = keep[zh] + got[zh]
    for k, out in ((1, one), (2, two), (3, three)):
        to = lax.rem(zh + k, 4)
        out[...] = (keep[to] + got[to]).astype(BF16)


def factor_kernel(place, mine, other, hidden, by_gate, by_up):
    zh, core = place[0], place[1]
    for k in range(4):
        group = lax.rem(zh + 4 - k, 4)
        first = jnp.where(core == 0, mine[k], other[k])
        second = jnp.where(core == 0, other[k], mine[k])
        for cut in range(CUTS):
            lanes = slice(cut * PART, (cut + 1) * PART)
            both = jnp.concatenate([first[:, :, lanes], second[:, :, lanes]], axis=2)
            for half in range(2):
                units = slice(half * HALF, (half + 1) * HALF)
                gate, up = both[0, units].astype(F32), both[1, units].astype(F32)
                sigma = jax.nn.sigmoid(gate)
                swish = gate * sigma
                hidden[cut, group, units] = (swish * up).astype(BF16)

                @pl.when(core == half)
                def _():
                    by_up[cut, group] = swish
                    by_gate[cut, group] = up * sigma * (1.0 + gate * (1.0 - sigma))


def back_kernel(place, mine, by_gate, by_up, out):
    zh = place[0]
    for k in range(4):
        group = lax.rem(zh + 4 - k, 4)
        block = mine[k].astype(F32)
        both = jnp.concatenate([block * by_gate[group], block * by_up[group]], axis=0)
        out[group, :, :448] = both.astype(BF16).T


def input_kernel(place, mine, other, gate_weight, up_weight, out):
    core = place[1]
    for n in range(4):
        columns = slice(n * 256, (n + 1) * 256)
        total = None
        for held, which in ((mine, core), (other, 1 - core)):
            units = pl.ds(pl.multiple_of(which * HALF, 32), HALF)
            right = jnp.concatenate([gate_weight[units, columns], up_weight[units, columns]], axis=0)
            left = held[:, :, :448].reshape(8 * PART, 448)
            term = jnp.dot(left, right, preferred_element_type=F32)
            total = term if total is None else total + term
        out[:, :, :, columns] = total.astype(BF16).reshape(4, 2, PART, 256)


def second_product(place, mine, other, gate_weight, up_weight):
    return call(
        input_kernel,
        shape(4, 2, PART, 1024, kind=BF16),
        (place, mine, other, gate_weight, up_weight),
    )


def momentum_kernel(*refs):
    slots, (hidden, momentum, direction, new_momentum) = refs[:CUTS], refs[CUTS:]
    total = None
    for cut in range(CUTS):
        left = jnp.concatenate([hidden[cut, zh ^ 2] for zh in range(4)], axis=1)
        term = jnp.dot(left, slots[cut][:, 0].reshape(8 * PART, 256), preferred_element_type=F32)
        total = term if total is None else total + term
    mean = total * 0.125
    direction[...] = (0.9 * momentum[...] + 0.1 * mean).astype(BF16)
    new_momentum[...] = 0.99 * momentum[...] + 0.01 * mean


def sum_kernel(slices, out, held, sems):
    copies = [
        pltpu.make_async_copy(slices.at[pl.ds(4 * i, 4)], held.at[pl.ds(4 * i, 4)], sems.at[i])
        for i in range(8)
    ]
    for copy in copies:
        copy.start()
    total = None
    for i, copy in enumerate(copies):
        copy.wait()
        for j in range(4 * i, 4 * i + 4):
            term = held[j].astype(F32)
            total = term if total is None else total + term
    out[...] = total.astype(BF16)


def exchange(slots, axes):
    return lax.all_to_all(slots, axes, split_axis=0, concat_axis=0, tiled=True)


def around(blocks):
    return [lax.ppermute(block, AXES, ALONG[k + 1]) for k, block in enumerate(blocks)]


def body(d_out, gate_act, up_act, gate_weight, up_weight, down_weight, momentum):
    place = jnp.stack([lax.axis_index("zh"), lax.axis_index("co")]).astype(jnp.int32)
    turned = lax.ppermute(d_out, AXES, TRANSPOSE)
    acts = jnp.stack([gate_act.T, up_act.T])
    if CUTS > 1:
        acts = acts.reshape(2, 448, 4, CUTS, ROWS).swapaxes(2, 3).reshape(2, 448, 128)
    acts, turned = lax.optimization_barrier((acts, turned))
    low = lax.axis_index("zl")
    beside = lax.ppermute(turned, AXES, NEXT_CHIP)
    pair = jnp.stack([jnp.where(low == 0, turned, beside), jnp.where(low == 0, beside, turned)])
    pair = pair.reshape(2, 4, CUTS, ROWS, 256)
    blocks = []
    for cut in range(CUTS):
        spread = jnp.broadcast_to(pair[:, :, cut].reshape(1, 2, PART, 256), (16, 2, PART, 256))
        blocks.append(exchange(spread, ("x", "y")).reshape(4, 4, 2, PART, 256))

    groups = around([acts] * 3)
    blocks[0], *groups = lax.optimization_barrier((blocks[0], *groups))
    mine = jnp.stack([acts] + groups)
    other = lax.ppermute(mine, AXES, OTHER_CORE)
    hidden, by_gate, by_up = call(
        factor_kernel,
        (
            shape(CUTS, 4, 448, 2 * PART, kind=BF16),
            shape(CUTS, 4, HALF, 2 * PART),
            shape(CUTS, 4, HALF, 2 * PART),
        ),
        (place, mine, other),
    )

    results = []
    for cut in range(CUTS):
        keep, give = first_product(place, blocks[cut], down_weight.T)
        got = lax.ppermute(give, AXES, OTHER_CORE)
        own, *away = call(
            split_kernel,
            (shape(HALF, 2 * PART),) + (shape(HALF, 2 * PART, kind=BF16),) * 3,
            (place, keep, got),
        )
        total = own
        for block in around(away):
            total = total + block.astype(F32)
        total = total.astype(BF16)
        mine = jnp.stack([total] + around([total] * 3))
        mine = call(
            back_kernel,
            shape(4, 2 * PART, 512, kind=BF16),
            (place, mine, by_gate[cut], by_up[cut]),
        )
        other = lax.ppermute(mine, AXES, OTHER_CORE)
        partial = second_product(place, mine, other, gate_weight.T, up_weight.T)
        slices = exchange(partial.reshape(32, ROWS, 1024), TENSOR)
        results.append(
            pl.pallas_call(
                sum_kernel,
                out_shape=shape(ROWS, 1024, kind=BF16),
                in_specs=[pl.BlockSpec(memory_space=pl.ANY)],
                scratch_shapes=[
                    pltpu.VMEM((32, ROWS, 1024), BF16),
                    pltpu.SemaphoreType.DMA((8,)),
                ],
                compiler_params=pltpu.CompilerParams(vmem_limit_bytes=LIMIT),
            )(slices)
        )
    d_in = jnp.concatenate(results, axis=0)

    direction, new_momentum = pl.pallas_call(
        momentum_kernel,
        grid=(4,),
        out_shape=(shape(448, 1024, kind=BF16), shape(448, 1024)),
        in_specs=[pl.BlockSpec((4, 1, 2, PART, 256), lambda y: (0, y, 0, 0, 0))] * CUTS
        + [
            pl.BlockSpec((CUTS, 4, 448, 2 * PART), lambda y: (0, 0, 0, 0)),
            pl.BlockSpec((448, 256), lambda y: (0, y)),
        ],
        out_specs=[pl.BlockSpec((448, 256), lambda y: (0, y))] * 2,
        compiler_params=pltpu.CompilerParams(vmem_limit_bytes=LIMIT),
    )(*blocks, hidden, momentum.T)
    return d_in, direction.T, new_momentum.T


def solution(mesh):
    fine = Mesh(mesh.devices.reshape(SIZES), AXES)
    both = P(DP, TENSOR)
    return jax.shard_map(
        body,
        mesh=fine,
        in_specs=(both,) * 7,
        out_specs=(P(TENSOR, DP), both, both),
        check_vma=False,
    )
```

```python
import jax
import jax.numpy as jnp
import numpy as np
from jax import lax
from jax.experimental import pallas as pl
from jax.experimental.pallas import tpu as pltpu
from jax.sharding import Mesh, PartitionSpec as P

AXES = ("zh", "co", "x", "zl", "y")
SIZES = (4, 2, 4, 2, 4)
DP = ("zh", "co")
TENSOR = ("x", "zl", "y")
F32, BF16 = jnp.float32, jnp.bfloat16
PLACE = pl.BlockSpec(memory_space=pltpu.SMEM)
WHOLE = pl.BlockSpec(memory_space=pltpu.VMEM)
LIMIT = 16 * 1024 * 1024


def pairs(move):
    found = []
    for source in range(256):
        place = [int(v) for v in np.unravel_index(source, SIZES)]
        found.append((source, int(np.ravel_multi_index(move(*place), SIZES))))
    return found


TRANSPOSE = pairs(lambda zh, co, x, zl, y: (x, co, (zh + 2) % 4, zl, y))
OTHER_CORE = pairs(lambda zh, co, x, zl, y: (zh, 1 - co, x, zl, y))
NEXT_CHIP = pairs(lambda zh, co, x, zl, y: (zh, co, x, 1 - zl, y))
ALONG = [pairs(lambda zh, co, x, zl, y, k=k: ((zh + k) % 4, co, x, zl, y)) for k in (1, 2, 3)]


def shape(*dims, kind=F32):
    return jax.ShapeDtypeStruct(dims, kind)


def call(kernel, out_shape, operands):
    return pl.pallas_call(
        kernel,
        out_shape=out_shape,
        in_specs=[PLACE] + [WHOLE] * (len(operands) - 1),
        out_specs=jax.tree.map(lambda _: WHOLE, out_shape),
        compiler_params=pltpu.CompilerParams(vmem_limit_bytes=LIMIT),
    )(*operands)


def product_kernel(place, slots, own_weight, other_weight, own, one, two, three, held, sems):
    core = place[1]
    copies = [
        pltpu.make_async_copy(
            slots.at[jnp.bitwise_xor(lax.rem(place[0] + k, 4), 2)], held.at[k], sems.at[k]
        )
        for k in range(4)
    ]
    for copy in copies:
        copy.start()
    turn = (((1,), (1,)), ((), ()))
    for k, outs in ((0, (own, one)), (2, (two, three))):
        copies[k].wait()
        copies[k + 1].wait()
        total = None
        for weight, which in ((own_weight, core), (other_weight, 1 - core)):
            for y in range(4):
                term = lax.dot_general(
                    weight[:, y * 256 : (y + 1) * 256],
                    held[k : k + 2, y, which].reshape(256, 256),
                    turn,
                    preferred_element_type=F32,
                )
                total = term if total is None else total + term
        for i, out in enumerate(outs):
            out[...] = total[:, i * 128 : (i + 1) * 128].astype(out.dtype)


def first_product(place, slots, own_weight, other_weight):
    return pl.pallas_call(
        product_kernel,
        out_shape=(shape(448, 128),) + (shape(448, 128, kind=BF16),) * 3,
        in_specs=[PLACE, pl.BlockSpec(memory_space=pl.ANY), WHOLE, WHOLE],
        out_specs=[WHOLE] * 4,
        scratch_shapes=[pltpu.VMEM((4, 4, 2, 128, 256), BF16), pltpu.SemaphoreType.DMA((4,))],
        compiler_params=pltpu.CompilerParams(vmem_limit_bytes=LIMIT),
    )(place, slots, own_weight, other_weight)


def factor_kernel(place, zero, one, two, three, hidden, by_gate, by_up):
    for k, held in enumerate((zero, one, two, three)):
        group = lax.rem(place[0] + 4 - k, 4)
        gate, up = held[0].astype(F32), held[1].astype(F32)
        sigma = jax.nn.sigmoid(gate)
        swish = gate * sigma
        hidden[group] = (swish * up).astype(BF16)
        by_up[group] = swish
        by_gate[group] = up * sigma * (1.0 + gate * (1.0 - sigma))


def back_kernel(place, zero, one, two, three, by_gate, by_up, out):
    for k, held in enumerate((zero, one, two, three)):
        group = lax.rem(place[0] + 4 - k, 4)
        block = held[...].astype(F32)
        both = jnp.concatenate([block * by_gate[group], block * by_up[group]], axis=0)
        out[group] = both.astype(BF16).T


def input_kernel(place, mine, other, gate_weight, up_weight, out):
    core = place[1]
    for n in range(4):
        columns = slice(n * 256, (n + 1) * 256)
        right = jnp.concatenate([gate_weight[:, columns], up_weight[:, columns]], axis=0)
        for held, which in ((mine, core), (other, 1 - core)):
            total = jnp.dot(held[...].reshape(512, 896), right, preferred_element_type=F32)
            for zh in range(4):
                out[zh, which, :, columns] = total[zh * 128 : (zh + 1) * 128].astype(BF16)


def momentum_kernel(place, slots, far, mine, other, momentum, direction, new_momentum):
    core = place[1]
    lefts = [mine[zh] for zh in range(4)] + [other[zh] for zh in range(4)]
    rights = [slots[zh ^ 2, 0, core] for zh in range(4)] + [far[zh ^ 2, 0] for zh in range(4)]
    total = jnp.dot(
        jnp.concatenate(lefts, axis=1), jnp.concatenate(rights, axis=0), preferred_element_type=F32
    )
    mean = total * 0.125
    direction[...] = (0.9 * momentum[...] + 0.1 * mean).astype(BF16)
    new_momentum[...] = 0.99 * momentum[...] + 0.01 * mean


def sum_kernel(slices, out, held, sems):
    copies = [
        pltpu.make_async_copy(slices.at[pl.ds(4 * i, 4)], held.at[pl.ds(4 * i, 4)], sems.at[i])
        for i in range(8)
    ]
    for copy in copies:
        copy.start()
    total = None
    for i, copy in enumerate(copies):
        copy.wait()
        for j in range(4 * i, 4 * i + 4):
            term = held[j].astype(F32)
            total = term if total is None else total + term
    out[...] = total.astype(BF16)


def exchange(slots, axes):
    return lax.all_to_all(slots, axes, split_axis=0, concat_axis=0, tiled=True)


def moved(block, route):
    return lax.ppermute(block, AXES, route)


def around(block):
    return [moved(block, route) for route in ALONG]


def body(d_out, gate_act, up_act, gate_weight, up_weight, down_weight, momentum):
    core = lax.axis_index("co")
    place = jnp.stack([lax.axis_index("zh"), core]).astype(jnp.int32)
    turned = moved(d_out, TRANSPOSE)
    acts = jnp.stack([gate_act.T, up_act.T])
    down_weight = down_weight.T
    down_other = moved(down_weight, OTHER_CORE)
    acts, turned, down_other = lax.optimization_barrier((acts, turned, down_other))
    beside = moved(turned, NEXT_CHIP)
    first = lax.axis_index("zl") == 0
    pair = jnp.stack([jnp.where(first, turned, beside), jnp.where(first, beside, turned)])
    slots = exchange(jnp.broadcast_to(pair[None], (16, 2, 128, 256)), ("x", "y"))
    slots = slots.reshape(4, 4, 2, 128, 256)
    groups = [acts] + around(acts)
    slots, *groups = lax.optimization_barrier((slots, *groups))

    own, *away = first_product(place, slots, down_weight, down_other)
    total = own
    for piece, route in zip(away, ALONG):
        total = total + moved(piece, route).astype(F32)
    total = total.astype(BF16)

    hidden, by_gate, by_up = call(
        factor_kernel,
        (shape(4, 448, 128, kind=BF16), shape(4, 448, 128), shape(4, 448, 128)),
        (place, *groups),
    )

    mine = call(
        back_kernel,
        shape(4, 128, 896, kind=BF16),
        (place, total, *around(total), by_gate, by_up),
    )
    other = moved(mine, OTHER_CORE)
    partial = call(
        input_kernel,
        shape(4, 2, 128, 1024, kind=BF16),
        (place, mine, other, gate_weight.T, up_weight.T),
    )
    slices = exchange(partial.reshape(32, 32, 1024), TENSOR)
    d_in = pl.pallas_call(
        sum_kernel,
        out_shape=shape(32, 1024, kind=BF16),
        in_specs=[pl.BlockSpec(memory_space=pl.ANY)],
        scratch_shapes=[pltpu.VMEM((32, 32, 1024), BF16), pltpu.SemaphoreType.DMA((8,))],
        compiler_params=pltpu.CompilerParams(vmem_limit_bytes=LIMIT),
    )(slices)

    hidden, slots, mine = lax.optimization_barrier((hidden, slots, mine))
    other = moved(hidden, OTHER_CORE)
    far = moved(lax.dynamic_index_in_dim(slots, 1 - core, 2, keepdims=False), OTHER_CORE)
    held = pl.BlockSpec((4, 448, 128), lambda y: (0, 0, 0))
    near = pl.BlockSpec((4, 1, 2, 128, 256), lambda y: (0, y, 0, 0, 0))
    some = pl.BlockSpec((4, 1, 128, 256), lambda y: (0, y, 0, 0))
    part = pl.BlockSpec((448, 256), lambda y: (0, y))
    direction, new_momentum = pl.pallas_call(
        momentum_kernel,
        grid=(4,),
        out_shape=(shape(448, 1024, kind=BF16), shape(448, 1024)),
        in_specs=[PLACE, near, some, held, held, part],
        out_specs=[part] * 2,
        compiler_params=pltpu.CompilerParams(vmem_limit_bytes=LIMIT),
    )(place, slots, far, hidden, other, momentum.T)
    return d_in, direction.T, new_momentum.T


def solution(mesh):
    fine = Mesh(mesh.devices.reshape(SIZES), AXES)
    both = P(DP, TENSOR)
    return jax.shard_map(
        body,
        mesh=fine,
        in_specs=(both,) * 7,
        out_specs=(P(TENSOR, DP), both, both),
        check_vma=False,
    )
```

```python
import functools

import jax
import jax.numpy as jnp
import numpy as np
from jax import lax
from jax.experimental import pallas as pl
from jax.experimental.pallas import tpu as pltpu
from jax.sharding import Mesh, PartitionSpec as P

AXES = ("zh", "co", "x", "zl", "y")
SIZES = (4, 2, 4, 2, 4)
DP = ("zh", "co")
TENSOR = ("x", "zl", "y")
F32, BF16 = jnp.float32, jnp.bfloat16
PLACE = pl.BlockSpec(memory_space=pltpu.SMEM)
WHOLE = pl.BlockSpec(memory_space=pltpu.VMEM)
LIMIT = 16 * 1024 * 1024


def pairs(move):
    found = []
    for source in range(256):
        place = [int(v) for v in np.unravel_index(source, SIZES)]
        found.append((source, int(np.ravel_multi_index(move(*place), SIZES))))
    return found


TRANSPOSE = pairs(lambda zh, co, x, zl, y: (x, co, (zh + 2) % 4, zl, y))
OTHER_CORE = pairs(lambda zh, co, x, zl, y: (zh, 1 - co, x, zl, y))
NEXT_CHIP = pairs(lambda zh, co, x, zl, y: (zh, co, x, 1 - zl, y))
ALONG = [pairs(lambda zh, co, x, zl, y, k=k: ((zh + k) % 4, co, x, zl, y)) for k in (1, 2, 3)]


def shape(*dims, kind=F32):
    return jax.ShapeDtypeStruct(dims, kind)


def call(kernel, out_shape, operands):
    return pl.pallas_call(
        kernel,
        out_shape=out_shape,
        in_specs=[PLACE] + [WHOLE] * (len(operands) - 1),
        out_specs=jax.tree.map(lambda _: WHOLE, out_shape),
        compiler_params=pltpu.CompilerParams(vmem_limit_bytes=LIMIT),
    )(*operands)


def product_kernel(place, slots, own_weight, other_weight, own, one, two, three, held, sems):
    core = place[1]
    copies = [
        pltpu.make_async_copy(
            slots.at[jnp.bitwise_xor(lax.rem(place[0] + k, 4), 2)], held.at[k], sems.at[k]
        )
        for k in range(4)
    ]
    for copy in copies:
        copy.start()
    turn = (((1,), (1,)), ((), ()))
    for k, outs in ((0, (own, one)), (2, (two, three))):
        copies[k].wait()
        copies[k + 1].wait()
        total = None
        for weight, which in ((own_weight, core), (other_weight, 1 - core)):
            for y in range(4):
                term = lax.dot_general(
                    weight[:, y * 256 : (y + 1) * 256],
                    held[k : k + 2, y, which].reshape(256, 256),
                    turn,
                    preferred_element_type=F32,
                )
                total = term if total is None else total + term
        for i, out in enumerate(outs):
            out[...] = total[:, i * 128 : (i + 1) * 128].astype(out.dtype)


def first_product(place, slots, own_weight, other_weight):
    return pl.pallas_call(
        product_kernel,
        out_shape=(shape(448, 128),) + (shape(448, 128, kind=BF16),) * 3,
        in_specs=[PLACE, pl.BlockSpec(memory_space=pl.ANY), WHOLE, WHOLE],
        out_specs=[WHOLE] * 4,
        scratch_shapes=[pltpu.VMEM((4, 4, 2, 128, 256), BF16), pltpu.SemaphoreType.DMA((4,))],
        compiler_params=pltpu.CompilerParams(vmem_limit_bytes=LIMIT),
    )(place, slots, own_weight, other_weight)


def factor_kernel(place, zero, one, two, three, hidden, by_gate, by_up):
    for k, held in enumerate((zero, one, two, three)):
        group = lax.rem(place[0] + 4 - k, 4)
        gate, up = held[0].astype(F32), held[1].astype(F32)
        sigma = jax.nn.sigmoid(gate)
        swish = gate * sigma
        hidden[group] = (swish * up).astype(BF16)
        by_up[group] = swish
        by_gate[group] = up * sigma * (1.0 + gate * (1.0 - sigma))


def back_kernel(place, zero, one, two, three, by_gate, by_up, out):
    for k, held in enumerate((zero, one, two, three)):
        group = lax.rem(place[0] + 4 - k, 4)
        block = held[...].astype(F32)
        both = jnp.concatenate([block * by_gate[group], block * by_up[group]], axis=0)
        out[group] = both.astype(BF16).T


def input_kernel(own, place, held, gate_weight, up_weight, *refs):
    out, part, sem = refs[-3:]
    which = place[1] if own else 1 - place[1]
    left = held[...].reshape(512, 896)
    for n in range(4):
        columns = slice(n * 256, (n + 1) * 256)
        right = jnp.concatenate([gate_weight[:, columns], up_weight[:, columns]], axis=0)
        total = jnp.dot(left, right, preferred_element_type=F32)
        part[:, :, columns] = total.astype(BF16).reshape(4, 128, 256)
    copy = pltpu.make_async_copy(part, out.at[:, which], sem)
    copy.start()
    copy.wait()


def second_product(own, place, held, gate_weight, up_weight, *filled):
    far = pl.BlockSpec(memory_space=pl.ANY)
    return pl.pallas_call(
        functools.partial(input_kernel, own),
        out_shape=shape(4, 2, 128, 1024, kind=BF16),
        in_specs=[PLACE] + [WHOLE] * 3 + [far] * len(filled),
        out_specs=far,
        scratch_shapes=[pltpu.VMEM((4, 128, 1024), BF16), pltpu.SemaphoreType.DMA],
        input_output_aliases={4: 0} if filled else {},
        compiler_params=pltpu.CompilerParams(vmem_limit_bytes=LIMIT),
    )(place, held, gate_weight, up_weight, *filled)


def momentum_kernel(place, slots, far, mine, other, momentum, direction, new_momentum):
    core = place[1]
    lefts = [mine[zh] for zh in range(4)] + [other[zh] for zh in range(4)]
    rights = [slots[zh ^ 2, 0, core] for zh in range(4)] + [far[zh ^ 2, 0] for zh in range(4)]
    total = jnp.dot(
        jnp.concatenate(lefts, axis=1), jnp.concatenate(rights, axis=0), preferred_element_type=F32
    )
    mean = total * 0.125
    direction[...] = (0.9 * momentum[...] + 0.1 * mean).astype(BF16)
    new_momentum[...] = 0.99 * momentum[...] + 0.01 * mean


def sum_kernel(slices, out, held, sems):
    copies = [
        pltpu.make_async_copy(slices.at[pl.ds(4 * i, 4)], held.at[pl.ds(4 * i, 4)], sems.at[i])
        for i in range(8)
    ]
    for copy in copies:
        copy.start()
    total = None
    for i, copy in enumerate(copies):
        copy.wait()
        for j in range(4 * i, 4 * i + 4):
            term = held[j].astype(F32)
            total = term if total is None else total + term
    out[...] = total.astype(BF16)


def exchange(slots, axes):
    return lax.all_to_all(slots, axes, split_axis=0, concat_axis=0, tiled=True)


def moved(block, route):
    return lax.ppermute(block, AXES, route)


def around(block):
    return [moved(block, route) for route in ALONG]


def body(d_out, gate_act, up_act, gate_weight, up_weight, down_weight, momentum):
    core = lax.axis_index("co")
    place = jnp.stack([lax.axis_index("zh"), core]).astype(jnp.int32)
    turned = moved(d_out, TRANSPOSE)
    acts = jnp.stack([gate_act.T, up_act.T])
    down_weight = down_weight.T
    down_other = moved(down_weight, OTHER_CORE)
    acts, turned, down_other = lax.optimization_barrier((acts, turned, down_other))
    beside = moved(turned, NEXT_CHIP)
    first = lax.axis_index("zl") == 0
    pair = jnp.stack([jnp.where(first, turned, beside), jnp.where(first, beside, turned)])
    slots = exchange(jnp.broadcast_to(pair[None], (16, 2, 128, 256)), ("x", "y"))
    slots = slots.reshape(4, 4, 2, 128, 256)
    groups = [acts] + around(acts)
    slots, *groups = lax.optimization_barrier((slots, *groups))

    own, *away = first_product(place, slots, down_weight, down_other)
    total = own
    for piece, route in zip(away, ALONG):
        total = total + moved(piece, route).astype(F32)
    total = total.astype(BF16)

    hidden, by_gate, by_up = call(
        factor_kernel,
        (shape(4, 448, 128, kind=BF16), shape(4, 448, 128), shape(4, 448, 128)),
        (place, *groups),
    )

    mine = call(
        back_kernel,
        shape(4, 128, 896, kind=BF16),
        (place, total, *around(total), by_gate, by_up),
    )
    other = moved(mine, OTHER_CORE)
    weights = gate_weight.T, up_weight.T
    partial = second_product(True, place, mine, *weights)
    partial = second_product(False, place, other, *weights, partial)
    slices = exchange(partial.reshape(32, 32, 1024), TENSOR)
    d_in = pl.pallas_call(
        sum_kernel,
        out_shape=shape(32, 1024, kind=BF16),
        in_specs=[pl.BlockSpec(memory_space=pl.ANY)],
        scratch_shapes=[pltpu.VMEM((32, 32, 1024), BF16), pltpu.SemaphoreType.DMA((8,))],
        compiler_params=pltpu.CompilerParams(vmem_limit_bytes=LIMIT),
    )(slices)

    hidden, slots, mine = lax.optimization_barrier((hidden, slots, mine))
    other = moved(hidden, OTHER_CORE)
    far = moved(lax.dynamic_index_in_dim(slots, 1 - core, 2, keepdims=False), OTHER_CORE)
    held = pl.BlockSpec((4, 448, 128), lambda y: (0, 0, 0))
    near = pl.BlockSpec((4, 1, 2, 128, 256), lambda y: (0, y, 0, 0, 0))
    some = pl.BlockSpec((4, 1, 128, 256), lambda y: (0, y, 0, 0))
    part = pl.BlockSpec((448, 256), lambda y: (0, y))
    direction, new_momentum = pl.pallas_call(
        momentum_kernel,
        grid=(4,),
        out_shape=(shape(448, 1024, kind=BF16), shape(448, 1024)),
        in_specs=[PLACE, near, some, held, held, part],
        out_specs=[part] * 2,
        compiler_params=pltpu.CompilerParams(vmem_limit_bytes=LIMIT),
    )(place, slots, far, hidden, other, momentum.T)
    return d_in, direction.T, new_momentum.T


def solution(mesh):
    fine = Mesh(mesh.devices.reshape(SIZES), AXES)
    both = P(DP, TENSOR)
    return jax.shard_map(
        body,
        mesh=fine,
        in_specs=(both,) * 7,
        out_specs=(P(TENSOR, DP), both, both),
        check_vma=False,
    )
```

```python
import functools

import jax
import jax.numpy as jnp
import numpy as np
from jax import lax
from jax.experimental import pallas as pl
from jax.experimental.pallas import tpu as pltpu
from jax.sharding import Mesh, PartitionSpec as P

AXES = ("zh", "co", "x", "zl", "y")
SIZES = (4, 2, 4, 2, 4)
DP = ("zh", "co")
TENSOR = ("x", "zl", "y")
F32, BF16 = jnp.float32, jnp.bfloat16
PLACE = pl.BlockSpec(memory_space=pltpu.SMEM)
WHOLE = pl.BlockSpec(memory_space=pltpu.VMEM)
LIMIT = 16 * 1024 * 1024


def pairs(move):
    found = []
    for source in range(256):
        place = [int(v) for v in np.unravel_index(source, SIZES)]
        found.append((source, int(np.ravel_multi_index(move(*place), SIZES))))
    return found


TRANSPOSE = pairs(lambda zh, co, x, zl, y: (x, co, (zh + 2) % 4, zl, y))
OTHER_CORE = pairs(lambda zh, co, x, zl, y: (zh, 1 - co, x, zl, y))
NEXT_CHIP = pairs(lambda zh, co, x, zl, y: (zh, co, x, 1 - zl, y))
ALONG = [pairs(lambda zh, co, x, zl, y, k=k: ((zh + k) % 4, co, x, zl, y)) for k in (1, 2, 3)]


def shape(*dims, kind=F32):
    return jax.ShapeDtypeStruct(dims, kind)


def call(kernel, out_shape, operands):
    return pl.pallas_call(
        kernel,
        out_shape=out_shape,
        in_specs=[PLACE] + [WHOLE] * (len(operands) - 1),
        out_specs=jax.tree.map(lambda _: WHOLE, out_shape),
        compiler_params=pltpu.CompilerParams(vmem_limit_bytes=LIMIT),
    )(*operands)


def product_kernel(place, slots, own_weight, other_weight, own, one, two, three, held, sems):
    core = place[1]
    copies = [
        pltpu.make_async_copy(
            slots.at[jnp.bitwise_xor(lax.rem(place[0] + k, 4), 2)], held.at[k], sems.at[k]
        )
        for k in range(4)
    ]
    for copy in copies:
        copy.start()
    turn = (((1,), (1,)), ((), ()))
    for k, outs in ((0, (own, one)), (2, (two, three))):
        copies[k].wait()
        copies[k + 1].wait()
        total = None
        for weight, which in ((own_weight, core), (other_weight, 1 - core)):
            for y in range(4):
                term = lax.dot_general(
                    weight[:, y * 256 : (y + 1) * 256],
                    held[k : k + 2, y, which].reshape(256, 256),
                    turn,
                    preferred_element_type=F32,
                )
                total = term if total is None else total + term
        for i, out in enumerate(outs):
            out[...] = total[:, i * 128 : (i + 1) * 128].astype(out.dtype)


def first_product(place, slots, own_weight, other_weight):
    return pl.pallas_call(
        product_kernel,
        out_shape=(shape(448, 128),) + (shape(448, 128, kind=BF16),) * 3,
        in_specs=[PLACE, pl.BlockSpec(memory_space=pl.ANY), WHOLE, WHOLE],
        out_specs=[WHOLE] * 4,
        scratch_shapes=[pltpu.VMEM((4, 4, 2, 128, 256), BF16), pltpu.SemaphoreType.DMA((4,))],
        compiler_params=pltpu.CompilerParams(vmem_limit_bytes=LIMIT),
    )(place, slots, own_weight, other_weight)


def factor_kernel(place, zero, one, two, three, hidden, by_gate, by_up):
    for k, held in enumerate((zero, one, two, three)):
        group = lax.rem(place[0] + 4 - k, 4)
        gate, up = held[0].astype(F32), held[1].astype(F32)
        sigma = jax.nn.sigmoid(gate)
        swish = gate * sigma
        hidden[group] = (swish * up).astype(BF16)
        by_up[group] = swish
        by_gate[group] = up * sigma * (1.0 + gate * (1.0 - sigma))


def back_kernel(place, zero, one, two, three, by_gate, by_up, out):
    for k, held in enumerate((zero, one, two, three)):
        group = lax.rem(place[0] + 4 - k, 4)
        block = held[...].astype(F32)
        both = jnp.concatenate([block * by_gate[group], block * by_up[group]], axis=0)
        out[group] = both.astype(BF16).T


def input_kernel(own, place, held, gate_weight, up_weight, *refs):
    out, part, sems = refs[-3:]
    copies = []
    which = place[1] if own else 1 - place[1]
    left = held[...].reshape(512, 896)
    for n in range(4):
        columns = slice(n * 256, (n + 1) * 256)
        right = jnp.concatenate([gate_weight[:, columns], up_weight[:, columns]], axis=0)
        total = jnp.dot(left, right, preferred_element_type=F32)
        part[n] = total.astype(BF16).reshape(4, 128, 256)
        copies.append(pltpu.make_async_copy(part.at[n], out.at[:, which, :, columns], sems.at[n]))
        copies[-1].start()
    for copy in copies:
        copy.wait()


def second_product(own, place, held, gate_weight, up_weight, *filled):
    far = pl.BlockSpec(memory_space=pl.ANY)
    return pl.pallas_call(
        functools.partial(input_kernel, own),
        out_shape=shape(4, 2, 128, 1024, kind=BF16),
        in_specs=[PLACE] + [WHOLE] * 3 + [far] * len(filled),
        out_specs=far,
        scratch_shapes=[pltpu.VMEM((4, 4, 128, 256), BF16), pltpu.SemaphoreType.DMA((4,))],
        input_output_aliases={4: 0} if filled else {},
        compiler_params=pltpu.CompilerParams(vmem_limit_bytes=LIMIT),
    )(place, held, gate_weight, up_weight, *filled)


def momentum_kernel(place, slots, far, mine, other, momentum, direction, new_momentum):
    core = place[1]
    lefts = [mine[zh] for zh in range(4)] + [other[zh] for zh in range(4)]
    rights = [slots[zh ^ 2, 0, core] for zh in range(4)] + [far[zh ^ 2, 0] for zh in range(4)]
    total = jnp.dot(
        jnp.concatenate(lefts, axis=1), jnp.concatenate(rights, axis=0), preferred_element_type=F32
    )
    mean = total * 0.125
    direction[...] = (0.9 * momentum[...] + 0.1 * mean).astype(BF16)
    new_momentum[...] = 0.99 * momentum[...] + 0.01 * mean


def sum_kernel(slices, out, held, sems):
    copies = [
        pltpu.make_async_copy(slices.at[pl.ds(4 * i, 4)], held.at[pl.ds(4 * i, 4)], sems.at[i])
        for i in range(8)
    ]
    for copy in copies:
        copy.start()
    total = None
    for i, copy in enumerate(copies):
        copy.wait()
        for j in range(4 * i, 4 * i + 4):
            term = held[j].astype(F32)
            total = term if total is None else total + term
    out[...] = total.astype(BF16)


def exchange(slots, axes):
    return lax.all_to_all(slots, axes, split_axis=0, concat_axis=0, tiled=True)


def moved(block, route):
    return lax.ppermute(block, AXES, route)


def around(block):
    return [moved(block, route) for route in ALONG]


def body(d_out, gate_act, up_act, gate_weight, up_weight, down_weight, momentum):
    core = lax.axis_index("co")
    place = jnp.stack([lax.axis_index("zh"), core]).astype(jnp.int32)
    turned = moved(d_out, TRANSPOSE)
    acts = jnp.stack([gate_act.T, up_act.T])
    down_weight = down_weight.T
    down_other = moved(down_weight, OTHER_CORE)
    acts, turned, down_other = lax.optimization_barrier((acts, turned, down_other))
    beside = moved(turned, NEXT_CHIP)
    first = lax.axis_index("zl") == 0
    pair = jnp.stack([jnp.where(first, turned, beside), jnp.where(first, beside, turned)])
    slots = exchange(jnp.broadcast_to(pair[None], (16, 2, 128, 256)), ("x", "y"))
    slots = slots.reshape(4, 4, 2, 128, 256)
    groups = [acts] + around(acts)
    slots, *groups = lax.optimization_barrier((slots, *groups))

    own, *away = first_product(place, slots, down_weight, down_other)
    total = own
    for piece, route in zip(away, ALONG):
        total = total + moved(piece, route).astype(F32)
    total = total.astype(BF16)

    hidden, by_gate, by_up = call(
        factor_kernel,
        (shape(4, 448, 128, kind=BF16), shape(4, 448, 128), shape(4, 448, 128)),
        (place, *groups),
    )

    mine = call(
        back_kernel,
        shape(4, 128, 896, kind=BF16),
        (place, total, *around(total), by_gate, by_up),
    )
    other = moved(mine, OTHER_CORE)
    weights = gate_weight.T, up_weight.T
    partial = second_product(True, place, mine, *weights)
    partial = second_product(False, place, other, *weights, partial)
    slices = exchange(partial.reshape(32, 32, 1024), TENSOR)
    d_in = pl.pallas_call(
        sum_kernel,
        out_shape=shape(32, 1024, kind=BF16),
        in_specs=[pl.BlockSpec(memory_space=pl.ANY)],
        scratch_shapes=[pltpu.VMEM((32, 32, 1024), BF16), pltpu.SemaphoreType.DMA((8,))],
        compiler_params=pltpu.CompilerParams(vmem_limit_bytes=LIMIT),
    )(slices)

    hidden, slots, mine = lax.optimization_barrier((hidden, slots, mine))
    other = moved(hidden, OTHER_CORE)
    far = moved(lax.dynamic_index_in_dim(slots, 1 - core, 2, keepdims=False), OTHER_CORE)
    held = pl.BlockSpec((4, 448, 128), lambda y: (0, 0, 0))
    near = pl.BlockSpec((4, 1, 2, 128, 256), lambda y: (0, y, 0, 0, 0))
    some = pl.BlockSpec((4, 1, 128, 256), lambda y: (0, y, 0, 0))
    part = pl.BlockSpec((448, 256), lambda y: (0, y))
    direction, new_momentum = pl.pallas_call(
        momentum_kernel,
        grid=(4,),
        out_shape=(shape(448, 1024, kind=BF16), shape(448, 1024)),
        in_specs=[PLACE, near, some, held, held, part],
        out_specs=[part] * 2,
        compiler_params=pltpu.CompilerParams(vmem_limit_bytes=LIMIT),
    )(place, slots, far, hidden, other, momentum.T)
    return d_in, direction.T, new_momentum.T


def solution(mesh):
    fine = Mesh(mesh.devices.reshape(SIZES), AXES)
    both = P(DP, TENSOR)
    return jax.shard_map(
        body,
        mesh=fine,
        in_specs=(both,) * 7,
        out_specs=(P(TENSOR, DP), both, both),
        check_vma=False,
    )
```
